32 devices in a mesh: groups: 1, pool: 32 (over z, y, x, core), tensor: 1.
Axes of the slice: x: 2, y: 2, z: 4, core: 2. Of those that a mesh axis runs over, the one named last changes fastest.
Arguments:
- hidden_input: bfloat16 [256, 8192], P(('groups', 'pool')), may hold values from -6 to 6
- key_value_weight: bfloat16 [8192, 2048], P('pool', 'tensor'), may hold values from -0.0625 to 0.0625
- adapter_down_weight: bfloat16 [32, 64, 8192], P('groups', 'tensor', 'pool'), may hold values from -0.0625 to 0.0625
- adapter_up_weight: bfloat16 [32, 64, 2048], P(('groups', 'pool'), None, 'tensor'), may hold values from -0.75 to 0.75
- adapter_of_row: int32 [256, 1], P('groups'), may hold values from 0 to 31
- adapter_page_table: int32 [32], P('groups'), may hold values from 0 to 31, each once
- cached_length: int32 [256], P(('groups', 'pool')), may hold values from 2 to 512, as said below
- queries: bfloat16 [256, 8192], P(('groups', 'pool'), 'tensor'), may hold values from -100 to 100
- key_value_cache: bfloat16 [256, 512, 2048], P(('groups', 'pool'), None, 'tensor'), may hold values from -4.5 to 4.5
Outputs:
- fresh_key_value: bfloat16 [256, 2048], P(('groups', 'pool'), 'tensor')
- attended: bfloat16 [256, 8192], P(('groups', 'pool'), 'tensor')
The draws below stay inside these ranges and needn't reach their ends.
Inputs may be any that keep to these rules, and one draw needn't show every extreme that they name: adapter_page_table[a] is the page of adapter a; pool index p holds page p. `adapter_of_row`: every adapter is used by some row. `cached_length`: some row of every replica holds the full 512.
All inputs are finite; a program needn't handle non-finite values.
Results may differ from the reference program's by a relative error of at most 0.0049.
Values may be sent and summed in bfloat16 or wider, within the bound.
A program may use at most 128 MiB of HBM per device.

```python
import math
import jax
import jax.numpy as jnp
from jax import lax

MODEL_WIDTH = 8192
QH = 64
KVH = 8
HD = 128
ADAPTER_RANK = 64
RD = 8
LMAX = 512
KEY_VALUE_COLS = 2048
ADAPTER_COUNT = 32
ROWS = 256
N_POOL = 32


def anchor_keys(key):
    return jnp.clip(jax.random.normal(key, (ROWS, KVH, HD), jnp.float32), -4.0, 4.0)


def draw_key_value_cache(key, part):
    anchor = anchor_keys(key)
    key = jax.random.fold_in(key, 3)
    stored = jnp.clip(jax.random.normal(key, (ROWS, LMAX, KVH, 2, HD), jnp.float32), -4.0, 4.0)
    stored = stored.at[:, 0, :, 0, :].set(anchor)
    return stored.reshape(ROWS, LMAX, KVH * 2 * HD).astype(jnp.bfloat16)


def draw_queries(key, part):
    key = jax.random.fold_in(key, 5)
    first_key = jax.random.fold_in(key, 0)
    group_size = QH // KVH
    values = jnp.clip(jax.random.normal(first_key, (ROWS, KVH, group_size, HD), jnp.float32), -4.0, 4.0)
    return values.reshape(ROWS, QH * HD).astype(jnp.bfloat16)


def draw_cached_length(key, part):
    key = jax.random.fold_in(key, 7)
    first_key, second_key = jax.random.split(key)
    first_draw = jax.random.randint(first_key, (ROWS,), 0, LMAX)
    second_draw = jax.random.randint(second_key, (ROWS,), 0, LMAX)
    lengths = 2 + first_draw * second_draw // LMAX
    return lengths.at[0].set(LMAX).astype(jnp.int32)


def block_scale(rng, dims, cuts, low, high):
    def one(dim, parts):
        steps = jax.random.uniform(jax.random.fold_in(jax.random.fold_in(rng, 6), dim), (parts,), jnp.float32, low / len(cuts), high / len(cuts))
        return jnp.repeat(jnp.exp(steps), dims[dim] // parts).reshape((-1,) + (1,) * (len(dims) - dim - 1))

    gain = one(*cuts[0])
    for cut in cuts[1:]:
        gain = gain * one(*cut)
    return gain


def different_ones(own_key, rows, count, top, lift):
    sequence = jax.random.permutation(jax.random.fold_in(own_key, 1), count)
    favour = sequence
    for power in range(3):
        favour = favour * favour // count
    favour = favour * lift // count
    tickets = jax.random.randint(jax.random.fold_in(own_key, 2), (rows, count), 0, 4096) + favour
    fixed_rows = jax.random.permutation(jax.random.fold_in(own_key, 3), rows)[jnp.arange(count) % rows]
    tickets = jnp.where(jnp.arange(rows)[:, None] == fixed_rows[None, :], 1 << 14, tickets)
    merit = tickets * count + jnp.arange(count)
    return lax.top_k(merit.astype(jnp.int32), top)[1].astype(jnp.int32)


def bell_draw(key, dims, width, limit, pieces=(), held_as=jnp.bfloat16):
    drawn = jax.random.normal(key, dims, jnp.float32) * width
    if len(pieces) > 0:
        drawn = block_scale(key, dims, pieces, -0.22, 0.18) * drawn
    return jnp.clip(drawn, min=-limit, max=limit).astype(held_as)


def setup_inputs(seed: int = 0, part: int = 0) -> dict:
    key_list = jax.random.split(jax.random.key(seed), 10)
    part_splits = jax.random.split(jax.random.fold_in(key_list[9], part), 10)
    return {
        "hidden_input": bell_draw(part_splits[0], (ROWS, MODEL_WIDTH), 1.0, 6.0, ((0, 32),)),
        "key_value_weight": bell_draw(key_list[1], (MODEL_WIDTH, KEY_VALUE_COLS), MODEL_WIDTH ** -0.5, 0.0625, ((0, 32),)),
        "adapter_down_weight": bell_draw(part_splits[2], (ADAPTER_COUNT, ADAPTER_RANK, MODEL_WIDTH), MODEL_WIDTH ** -0.5, 0.0625, ((2, 32),)),
        "adapter_up_weight": bell_draw(part_splits[3], (ADAPTER_COUNT, ADAPTER_RANK, KEY_VALUE_COLS), ADAPTER_RANK ** -0.5, 0.75, ((0, 32),)),
        "adapter_of_row": different_ones(part_splits[4], ROWS, ADAPTER_COUNT, 1, 512),
        "adapter_page_table": jax.random.permutation(part_splits[5], ADAPTER_COUNT).astype(jnp.int32),
        "cached_length": draw_cached_length(jax.random.fold_in(jax.random.fold_in(key_list[9], part), 71), part),
        "queries": draw_queries(jax.random.fold_in(jax.random.fold_in(key_list[9], part), 71), part),
        "key_value_cache": draw_key_value_cache(jax.random.fold_in(jax.random.fold_in(key_list[9], part), 71), part),
    }


ADAPTER_SCALE = 0.5

def attend_rows(query_block, stored, new_kv, lengths):
    query_f = query_block.astype(jnp.float32)
    cache_keys = stored[:, :, :, 0, :].astype(jnp.float32)
    cache_vals = stored[:, :, :, 1, :].astype(jnp.float32)
    inv_root = 1.0 / math.sqrt(query_block.shape[-1])
    scores = jnp.einsum('rkgd,rlkd->rkgl', query_f, cache_keys) * inv_root
    own_score = jnp.einsum('rkgd,rkd->rkg', query_f, new_kv[:, :, 0, :].astype(jnp.float32)) * inv_root
    positions = jnp.arange(stored.shape[1]).astype(jnp.int32)
    in_cache = positions[None, None, None, :] < lengths.astype(jnp.int32)[:, None, None, None]
    scores = jnp.where(in_cache, scores, -jnp.inf)
    peak = jnp.maximum(lax.optimization_barrier(jnp.max(scores, axis=-1)), own_score)
    weights = jnp.exp(scores - peak[..., None])
    own_weight = jnp.exp(own_score - peak)
    weight_sum = lax.optimization_barrier(jnp.sum(weights, axis=-1)) + own_weight
    weights_b = lax.optimization_barrier(weights.astype(jnp.bfloat16))
    own_b = lax.optimization_barrier(own_weight.astype(jnp.bfloat16))
    mixture = jnp.einsum('rkgl,rlkd->rkgd', weights_b.astype(jnp.float32), cache_vals)
    new_vals = new_kv[:, :, 1, :].astype(jnp.float32)
    mixture = mixture + own_b.astype(jnp.float32)[..., None] * new_vals[:, :, None, :]
    return (mixture / weight_sum[..., None]).astype(jnp.bfloat16)

def reference(hidden_input, key_value_weight, adapter_down_weight, adapter_up_weight, adapter_of_row, adapter_page_table, cached_length, queries, key_value_cache):
    base_output = jnp.dot(hidden_input, key_value_weight, preferred_element_type=jnp.float32)
    adapter_list = adapter_of_row[:, 0].astype(jnp.int32)
    flattened_down = adapter_down_weight.reshape(ADAPTER_COUNT * ADAPTER_RANK, MODEL_WIDTH)
    every_rank = jnp.dot(hidden_input, flattened_down.T, preferred_element_type=jnp.float32).reshape(ROWS, ADAPTER_COUNT, ADAPTER_RANK)
    rank_vec = jnp.take_along_axis(every_rank, adapter_list[:, None, None], axis=1)[:, 0, :].astype(jnp.bfloat16)
    slot_ids = jnp.take(adapter_page_table, adapter_list).astype(jnp.int32)

    def expand(pair):
        rank_rows, row_page_slots = pair
        selected_down = jnp.take(adapter_up_weight, row_page_slots, axis=0).astype(jnp.float32)
        return jnp.einsum('rk,rkc->rc', rank_rows.astype(jnp.float32), selected_down)
    adapter_delta = lax.map(expand, (rank_vec.reshape(N_POOL, RD, ADAPTER_RANK), slot_ids.reshape(N_POOL, RD))).reshape(ROWS, KEY_VALUE_COLS)
    fresh_key_value = (base_output + ADAPTER_SCALE * adapter_delta).astype(jnp.bfloat16)
    group_size = QH // KVH
    query_blocks = queries.reshape(N_POOL, RD, KVH, group_size, HD)
    cache_blocks = key_value_cache.reshape(N_POOL, RD, LMAX, KVH, 2, HD)
    new_blocks = fresh_key_value.reshape(N_POOL, RD, KVH, 2, HD)
    length_blocks = cached_length.reshape(N_POOL, RD)

    def one_block(quad):
        return attend_rows(quad[0], quad[1], quad[2], quad[3])
    attended = lax.map(one_block, (query_blocks, cache_blocks, new_blocks, length_blocks)).reshape(ROWS, QH * HD)
    return (fresh_key_value, attended)
```

```python
import functools
import math

import jax
import jax.numpy as jnp
from jax import lax
from jax.experimental import pallas as pl
from jax.experimental.pallas import tpu as pltpu
from jax.sharding import PartitionSpec as P

QH = 64
KVH = 8
HD = 128
GROUP = QH // KVH
LANES = 128
ADAPTER_SCALE = 0.5
MESH = pl.DeviceIdType.MESH
BF16 = jnp.bfloat16
F32 = jnp.float32


def stage_plan(pool, cols):
    bits = pool.bit_length() - 1
    plain = list(range(bits))
    other = [0, 2, 1] + plain[3:]
    half = cols // 2
    return [(0, half, plain), (half, cols - half, other)]


def stage_type(stage):
    return BF16 if stage < 3 else F32


def slot_of(d, order):
    bits = len(order)
    return sum(((d >> b) & 1) << (bits - 1 - j) for j, b in enumerate(order))


def kernel(pool, tensor, rd, feats, cols, rank, lmax, heads, *refs):
    bits = pool.bit_length() - 1
    plan = stage_plan(pool, cols)
    groups = len(plan)
    refs = list(refs)
    hidden, ids_ref, pages_ref, lens_ref, q_ref, w_hbm, down_hbm, up_hbm, cache_hbm = refs[:9]
    fresh_ref, att_ref = refs[9:11]
    (xs, xg, xm, w_v, down_v, up_v, kv, qs, o_acc, m_acc, l_acc, rk, rr, rs, rv) = refs[11:26]
    rest = refs[26:]
    acc = rest[:groups]
    rest = rest[groups:]
    sbuf = [[rest[(g * bits + j) * 2] for j in range(bits)] for g in range(groups)]
    rbuf = [[rest[(g * bits + j) * 2 + 1] for j in range(bits)] for g in range(groups)]
    rest = rest[2 * groups * bits:]
    lsem, kvsem, s1, r1, s2, r2, s3, r3, s4, r4 = rest

    me = lax.axis_index("pool")
    mt = lax.axis_index("tensor")
    rows = pool * rd
    copies_up = LANES // rank

    local = [
        pltpu.make_async_copy(down_hbm, down_v, lsem.at[0]),
        pltpu.make_async_copy(w_hbm, w_v, lsem.at[1]),
    ]
    ups = []
    for t in range(tensor):
        for i in range(copies_up):
            ups.append(
                pltpu.make_async_copy(
                    up_hbm.at[pl.ds(t * rank, rank)],
                    up_v.at[t, pl.ds(i * rank, rank)],
                    lsem.at[2 + t * copies_up + i],
                )
            )
    kvs = [pltpu.make_async_copy(cache_hbm.at[r], kv.at[r], kvsem.at[r]) for r in range(rd)]
    for c in local + ups + kvs:
        c.start()

    barrier = pltpu.get_barrier_semaphore()
    for to in range(tensor):
        tt = lax.rem(mt + to, tensor)

        def greet(k, carry, tt=tt):
            pl.semaphore_signal(
                barrier, inc=1, device_id={"pool": lax.rem(me + k, pool), "tensor": tt}, device_id_type=MESH
            )
            return carry

        lax.fori_loop(1 if to == 0 else 0, pool, greet, 0)

    for d in range(pool):
        xs[d] = hidden[:, d * feats:(d + 1) * feats]
    xg[me] = xs[me]
    pl.semaphore_wait(barrier, pool * tensor - 1)

    def hid_copy(k, to, slot):
        return pltpu.make_async_remote_copy(
            src_ref=xs.at[to], dst_ref=xg.at[slot], send_sem=s1.at[k], recv_sem=r1.at[k],
            device_id={"pool": to}, device_id_type=MESH,
        )

    def rank_copy(k, to, slot):
        return pltpu.make_async_remote_copy(
            src_ref=rk.at[to], dst_ref=rr.at[slot], send_sem=s2.at[k], recv_sem=r2.at[k],
            device_id={"pool": to}, device_id_type=MESH,
        )

    def vec_copy(off, k, to, tt, slot, ts):
        return pltpu.make_async_remote_copy(
            src_ref=rs, dst_ref=rv.at[ts, slot], send_sem=s3.at[off, k], recv_sem=r3.at[off, k],
            device_id={"pool": to, "tensor": tt}, device_id_type=MESH,
        )

    def each(first, fn):
        def step(k, carry):
            fn(k, lax.rem(me + k, pool), lax.rem(me + pool - k, pool))
            return carry

        lax.fori_loop(first, pool, step, 0)

    each(1, lambda k, to, frm: hid_copy(k, to, me).start())

    nq = heads * GROUP
    for j in range(nq):
        qs[pl.ds(j, rd, stride=nq), :] = q_ref[:, j * HD:(j + 1) * HD].astype(F32)
    inv_root = 1.0 / math.sqrt(HD)

    def attend(r0, r1_):
        for r in range(r0, r1_):
            kvs[r].wait()

        def row(r, carry):
            live = lax.broadcasted_iota(jnp.int32, (nq, lmax), 1) < lens_ref[r]
            q_row = qs[pl.ds(pl.multiple_of(r * nq, nq), nq), :].astype(BF16)
            parts = []
            for h in range(heads):
                k_h = kv[r, :, 2 * h * HD:(2 * h + 1) * HD]
                parts.append(
                    lax.dot_general(
                        q_row[h * GROUP:(h + 1) * GROUP], k_h, (((1,), (1,)), ((), ())),
                        preferred_element_type=F32,
                    )
                )
            s = jnp.concatenate(parts, axis=0) * inv_root
            s = jnp.where(live, s, -jnp.inf)
            m = jnp.max(s, axis=-1, keepdims=True)
            p = jnp.exp(s - m)
            l = jnp.sum(p, axis=-1, keepdims=True)
            pb = p.astype(BF16)
            outs = []
            for h in range(heads):
                v_h = kv[r, :, (2 * h + 1) * HD:(2 * h + 2) * HD]
                outs.append(
                    jnp.dot(pb[h * GROUP:(h + 1) * GROUP], v_h, preferred_element_type=F32)
                )
            at = pl.ds(pl.multiple_of(r * nq, nq), nq)
            o_acc[at, :] = jnp.concatenate(outs, axis=0)
            m_acc[at, :] = jnp.broadcast_to(m, (nq, LANES))
            l_acc[at, :] = jnp.broadcast_to(l, (nq, LANES))
            return carry

        lax.fori_loop(r0, r1_, row, 0)

    local[0].wait()
    attend(0, 2)

    each(1, lambda k, to, frm: hid_copy(k, to, frm).wait_recv())
    xm[...] = xg[...].astype(F32).reshape(rows, feats).astype(BF16)
    ids = ids_ref[...]
    total = jnp.zeros((rows, LANES), F32)
    lane_sub = lax.broadcasted_iota(jnp.int32, (rows, LANES), 1) // rank
    for c in range(down_v.shape[0] // LANES):
        y = lax.dot_general(
            xm[...], down_v[c * LANES:(c + 1) * LANES, :], (((1,), (1,)), ((), ())),
            preferred_element_type=F32,
        )
        total = total + jnp.where(lane_sub + c * copies_up == ids, y, 0.0)
    rk[...] = total.reshape(pool, rd, LANES)
    rr[me] = rk[me]
    each(1, lambda k, to, frm: rank_copy(k, to, me).start())

    attend(2, 4)

    each(1, lambda k, to, frm: rank_copy(k, to, frm).wait_recv())
    mine = jnp.sum(rr[...], axis=0).astype(BF16)
    rs[...] = mine
    rv[mt, me] = mine
    for off in range(tensor):
        tt = lax.rem(mt + off, tensor)
        each(1 if off == 0 else 0, lambda k, to, frm: vec_copy(off, k, to, tt, me, mt).start())

    attend(4, 6)

    for c in local[1:] + ups:
        c.wait()
    for off in range(tensor):
        tf = lax.rem(mt + tensor - off, tensor)
        each(1 if off == 0 else 0, lambda k, to, frm: vec_copy(off, k, to, mt, frm, tf).wait_recv())
    pages = pages_ref[...]
    my_adapter = jnp.sum(
        jnp.where(pages == me, lax.broadcasted_iota(jnp.int32, pages.shape, 1), 0), axis=1, keepdims=True
    )
    held = ids == my_adapter
    vecs = [
        jnp.where(held, rv[t].astype(F32).reshape(rows, LANES), 0.0).astype(BF16) for t in range(tensor)
    ]
    width = 256

    def piece(g, j):
        half = pool >> (j + 1)
        bit = plan[g][2][j]
        partner_bit = lax.rem(me // (1 << bit), 2)
        partner = me + (1 - 2 * partner_bit) * (1 << bit)
        copy = pltpu.make_async_remote_copy(
            src_ref=sbuf[g][j], dst_ref=rbuf[g][j], send_sem=s4.at[g, j], recv_sem=r4.at[g, j],
            device_id={"pool": partner}, device_id_type=MESH,
        )
        return half, partner_bit, copy

    offs = [0] * groups
    sent = []
    for g, (c0, cn, order) in enumerate(plan):
        for c in range(0, cn, width):
            at = slice(c0 + c, c0 + c + width)
            part = jnp.dot(xm[...], w_v[:, at], preferred_element_type=F32)
            for t in range(tensor):
                part = part + ADAPTER_SCALE * jnp.dot(vecs[t], up_v[t, :, at], preferred_element_type=F32)
            for d in range(pool):
                acc[g][slot_of(d, order), :, c:c + width] = part[d * rd:(d + 1) * rd]
        half, b, copy = piece(g, 0)
        sbuf[g][0][...] = acc[g][pl.ds((1 - b) * half, half)].astype(stage_type(0))
        copy.start()
        sent.append(copy)
        offs[g] = b * half
    cuts = {1: (6, 7), 2: (7, 8)}
    for j in range(1, bits):
        if j in cuts:
            attend(*cuts[j])
        for g in range(groups):
            piece(g, j - 1)[2].wait_recv()
            half, b, copy = piece(g, j)
            away, keep = (1 - b) * half, b * half
            sbuf[g][j][...] = (
                acc[g][pl.ds(offs[g] + away, half)] + rbuf[g][j - 1][pl.ds(away, half)].astype(F32)
            ).astype(stage_type(j))
            copy.start()
            sent.append(copy)
            acc[g][pl.ds(offs[g] + keep, half)] += rbuf[g][j - 1][pl.ds(keep, half)].astype(F32)
            offs[g] = offs[g] + keep
    for g, (c0, cn, order) in enumerate(plan):
        piece(g, bits - 1)[2].wait_recv()
        fresh_ref[:, c0:c0 + cn] = (acc[g][offs[g]] + rbuf[g][bits - 1][0].astype(F32)).astype(BF16)

    for h in range(heads):
        new_k = fresh_ref[:, 2 * h * HD:(2 * h + 1) * HD].astype(F32)
        new_v = fresh_ref[:, (2 * h + 1) * HD:(2 * h + 2) * HD].astype(F32)
        for gq in range(GROUP):
            j = h * GROUP + gq
            at = pl.ds(j, rd, stride=nq)
            own = jnp.sum(qs[at, :] * new_k, axis=-1, keepdims=True) * inv_root
            m = m_acc[at, :]
            peak = jnp.maximum(m, own)
            old_w = jnp.exp(m - peak)
            own_w = jnp.exp(own - peak)
            total_w = l_acc[at, :] * old_w + own_w
            mix = o_acc[at, :] * old_w + own_w.astype(BF16).astype(F32) * new_v
            att_ref[:, j * HD:(j + 1) * HD] = (mix / total_w).astype(BF16)

    each(1, lambda k, to, frm: hid_copy(k, to, me).wait_send())
    each(1, lambda k, to, frm: rank_copy(k, to, me).wait_send())
    for off in range(tensor):
        tt = lax.rem(mt + off, tensor)
        each(1 if off == 0 else 0, lambda k, to, frm: vec_copy(off, k, to, tt, me, mt).wait_send())
    for c in sent:
        c.wait_send()


def body(pool, tensor, hidden, kv_w, down, up, ids, pages, lens, queries, cache):
    rd, width = hidden.shape
    feats, cols = kv_w.shape
    adapters, rank, _ = down.shape
    lmax = cache.shape[1]
    heads = cols // (2 * HD)
    bits = pool.bit_length() - 1
    plan = stage_plan(pool, cols)
    dma = pltpu.SemaphoreType.DMA
    vm = pltpu.VMEM
    nq = heads * GROUP
    scratch = [
        vm((pool, rd, feats), BF16),
        vm((pool, rd, feats), BF16),
        vm((pool * rd, feats), BF16),
        vm((feats, cols), BF16),
        vm((adapters * rank, feats), BF16),
        vm((tensor, LANES, cols), BF16),
        vm((rd, lmax, cols), BF16),
        vm((rd * nq, HD), F32),
        vm((rd * nq, HD), F32),
        vm((rd * nq, LANES), F32),
        vm((rd * nq, LANES), F32),
        vm((pool, rd, LANES), F32),
        vm((pool, rd, LANES), F32),
        vm((rd, LANES), BF16),
        vm((tensor, pool, rd, LANES), BF16),
    ]
    scratch += [vm((pool, rd, cn), F32) for _, cn, _ in plan]
    for _, cn, _ in plan:
        for j in range(bits):
            scratch += [vm((pool >> (j + 1), rd, cn), stage_type(j))] * 2
    scratch += [
        dma((2 + tensor * (LANES // rank),)),
        dma((rd,)),
        dma((pool,)), dma((pool,)),
        dma((pool,)), dma((pool,)),
        dma((tensor, pool)), dma((tensor, pool)),
        dma((len(plan), bits)), dma((len(plan), bits)),
    ]
    vspec = pl.BlockSpec(memory_space=pltpu.VMEM)
    hbm = pl.BlockSpec(memory_space=pl.ANY)
    return pl.pallas_call(
        functools.partial(kernel, pool, tensor, rd, feats, cols, rank, lmax, heads),
        out_shape=(
            jax.ShapeDtypeStruct((rd, cols), BF16),
            jax.ShapeDtypeStruct((rd, queries.shape[1]), BF16),
        ),
        in_specs=[vspec, vspec, vspec, pl.BlockSpec(memory_space=pltpu.SMEM), vspec, hbm, hbm, hbm, hbm],
        out_specs=(vspec, vspec),
        scratch_shapes=scratch,
        compiler_params=pltpu.CompilerParams(
            collective_id=0, has_side_effects=True, vmem_limit_bytes=52 * 1024 * 1024
        ),
    )(
        hidden, ids, pages.reshape(1, -1), lens, queries,
        kv_w, down.reshape(adapters * rank, feats), up.reshape(up.shape[1], cols), cache,
    )


def solution(mesh):
    in_specs = (
        P(("groups", "pool"), None),
        P("pool", "tensor"),
        P("groups", "tensor", "pool"),
        P(("groups", "pool"), None, "tensor"),
        P("groups", None),
        P("groups"),
        P(("groups", "pool")),
        P(("groups", "pool"), "tensor"),
        P(("groups", "pool"), None, "tensor"),
    )
    out_specs = (P(("groups", "pool"), "tensor"), P(("groups", "pool"), "tensor"))
    fn = functools.partial(body, mesh.shape["pool"], mesh.shape["tensor"])
    return jax.shard_map(fn, mesh=mesh, in_specs=in_specs, out_specs=out_specs, check_vma=False)
```

```python
import functools
import math

import jax
import jax.numpy as jnp
from jax import lax
from jax.experimental import pallas as pl
from jax.experimental.pallas import tpu as pltpu
from jax.sharding import PartitionSpec as P

QH = 64
KVH = 8
HD = 128
GROUP = QH // KVH
LANES = 128
ADAPTER_SCALE = 0.5
MESH = pl.DeviceIdType.MESH
BF16 = jnp.bfloat16
F32 = jnp.float32


def orders():
    return ((1, 2), (2, 1))


def kernel(pool, tensor, rd, feats, cols, rank, lmax, heads, *refs):
    hidden, ids_hbm, pages_hbm, lens_hbm, q_hbm, w_hbm, down_hbm, up_hbm, cache_hbm = refs[:9]
    fresh_ref, att_ref = refs[9:11]
    (xg, xm, w_v, down_v, up_v, kv, q_ref, ids_raw, pages_ref, lens_ref, ids3, qs, o_acc, m_acc, l_acc,
     rk, rr, rs, rv, base, s0, t0) = refs[11:33]
    groups = len(orders())
    gw = cols // groups
    per = 7
    bufs = [refs[33 + g * per:33 + (g + 1) * per] for g in range(groups)]
    (lsem, kvsem, usem, vsem, s1, r1, s2, r2, s3, r3, sp, rp, sx, rx, sy, ry, sz, rz) = refs[33 + groups * per:]

    me = lax.axis_index("pool")
    mt = lax.axis_index("tensor")
    rows = pool * rd
    half, quarter, eighth = pool // 2, pool // 4, pool // 8
    copies_up = LANES // rank
    hr = half * rd

    def bit_of(d, b):
        return lax.rem(d // (1 << b), 2)

    def partner_of(b):
        return me + (1 - 2 * bit_of(me, b)) * (1 << b)

    core = bit_of(me, 0)

    def slot(d):
        return lax.rem(d, 2) * half + d // 2

    barrier = pltpu.get_barrier_semaphore()
    for to in range(tensor):
        tt = lax.rem(mt + to, tensor)

        def greet(k, carry, tt=tt):
            pl.semaphore_signal(
                barrier, inc=1, device_id={"pool": lax.rem(me + k, pool), "tensor": tt}, device_id_type=MESH
            )
            return carry

        lax.fori_loop(1 if to == 0 else 0, pool, greet, 0)

    def hidden_cols(d):
        return hidden.at[:, pl.ds(pl.multiple_of(d * feats, feats), feats)]

    own_x = pltpu.make_async_copy(hidden_cols(me), xg.at[slot(me)], lsem.at[0])
    c_q = pltpu.make_async_copy(q_hbm, q_ref, lsem.at[1])
    c_ids = pltpu.make_async_copy(ids_hbm, ids_raw, lsem.at[2])
    c_pages = pltpu.make_async_copy(pages_hbm, pages_ref, lsem.at[3])
    c_lens = pltpu.make_async_copy(lens_hbm, lens_ref, lsem.at[4])
    c_down = pltpu.make_async_copy(down_hbm, down_v, lsem.at[5])
    c_w = pltpu.make_async_copy(w_hbm, w_v, lsem.at[6])
    ups = []
    pups = []
    for t in range(tensor):
        for i in range(copies_up):
            src = up_hbm.at[pl.ds(t * rank, rank)]
            n = t * copies_up + i
            ups.append(pltpu.make_async_copy(src, up_v.at[0, t, pl.ds(i * rank, rank)], usem.at[n]))
            pups.append(
                pltpu.make_async_remote_copy(
                    src_ref=src, dst_ref=up_v.at[1, t, pl.ds(i * rank, rank)],
                    send_sem=sp.at[n], recv_sem=rp.at[n],
                    device_id={"pool": partner_of(0)}, device_id_type=MESH,
                )
            )
    kvs = [pltpu.make_async_copy(cache_hbm.at[r], kv.at[r], kvsem.at[r]) for r in range(rd)]
    for c in [own_x, c_q, c_ids, c_pages, c_lens, c_down, c_w] + kvs[:2] + ups + kvs[2:]:
        c.start()

    pl.semaphore_wait(barrier, pool * tensor - 1)

    def hid_copy(k, to, at):
        return pltpu.make_async_remote_copy(
            src_ref=hidden_cols(to), dst_ref=xg.at[at], send_sem=s1.at[k], recv_sem=r1.at[k],
            device_id={"pool": to}, device_id_type=MESH,
        )

    def rank_copy(k, to, at):
        return pltpu.make_async_remote_copy(
            src_ref=rk.at[slot(to)], dst_ref=rr.at[at], send_sem=s2.at[k], recv_sem=r2.at[k],
            device_id={"pool": to}, device_id_type=MESH,
        )

    def vec_copy(off, k, to, tt, at, ts):
        return pltpu.make_async_remote_copy(
            src_ref=rs, dst_ref=rv.at[ts, at], send_sem=s3.at[off, k], recv_sem=r3.at[off, k],
            device_id={"pool": to, "tensor": tt}, device_id_type=MESH,
        )

    def each(first, fn, count=pool, stride=1):
        def step(k, carry):
            fn(k, lax.rem(me + k * stride, pool), lax.rem(me + pool - k * stride, pool))
            return carry

        lax.fori_loop(first, count, step, 0)

    each(1, lambda k, to, frm: hid_copy(k, to, slot(me)).start())
    for c in pups:
        c.start()

    nq = heads * GROUP
    c_q.wait()
    for j in range(nq):
        qs[pl.ds(j, rd, stride=nq), :] = q_ref[:, j * HD:(j + 1) * HD].astype(F32)
    inv_root = 1.0 / math.sqrt(HD)
    c_ids.wait()
    ids_t = jnp.broadcast_to(ids_raw[...], (LANES, rows)).T
    for d in range(pool):
        ids3[(d % 2) * half + d // 2] = ids_t[d * rd:(d + 1) * rd]
    c_pages.wait()
    c_lens.wait()

    def attend(r0, r1_):
        for r in range(r0, r1_):
            kvs[r].wait()

        def row(r, carry):
            live = lax.broadcasted_iota(jnp.int32, (nq, lmax), 1) < lens_ref[r]
            q_row = qs[pl.ds(pl.multiple_of(r * nq, nq), nq), :].astype(BF16)
            parts = []
            for h in range(heads):
                k_h = kv[r, :, 2 * h * HD:(2 * h + 1) * HD]
                parts.append(
                    lax.dot_general(
                        q_row[h * GROUP:(h + 1) * GROUP], k_h, (((1,), (1,)), ((), ())),
                        preferred_element_type=F32,
                    )
                )
            s = jnp.concatenate(parts, axis=0) * inv_root
            s = jnp.where(live, s, -jnp.inf)
            m = jnp.max(s, axis=-1, keepdims=True)
            p = jnp.exp(s - m)
            l = jnp.sum(p, axis=-1, keepdims=True)
            pb = p.astype(BF16)
            outs = []
            for h in range(heads):
                v_h = kv[r, :, (2 * h + 1) * HD:(2 * h + 2) * HD]
                outs.append(
                    jnp.dot(pb[h * GROUP:(h + 1) * GROUP], v_h, preferred_element_type=F32)
                )
            at = pl.ds(pl.multiple_of(r * nq, nq), nq)
            o_acc[at, :] = jnp.concatenate(outs, axis=0)
            m_acc[at, :] = jnp.broadcast_to(m, (nq, LANES))
            l_acc[at, :] = jnp.broadcast_to(l, (nq, LANES))
            return carry

        lax.fori_loop(r0, r1_, row, 0)

    c_down.wait()
    c_w.wait()
    attend(0, 2)

    own_x.wait()
    each(1, lambda k, to, frm: hid_copy(k, to, slot(frm)).wait_recv())
    xm[...] = xg[...].astype(F32).reshape(rows, feats).astype(BF16)
    ids = ids3[...].reshape(rows, LANES)
    total = jnp.zeros((rows, LANES), F32)
    lane_sub = lax.broadcasted_iota(jnp.int32, (rows, LANES), 1) // rank
    for c in range(down_v.shape[0] // LANES):
        y = lax.dot_general(
            xm[...], down_v[c * LANES:(c + 1) * LANES, :], (((1,), (1,)), ((), ())),
            preferred_element_type=F32,
        )
        total = total + jnp.where(lane_sub + c * copies_up == ids, y, 0.0)
    rk[...] = total.reshape(pool, rd, LANES).astype(BF16)
    rr[me] = rk[slot(me)]
    each(1, lambda k, to, frm: rank_copy(k, to, me).start())

    width = 256
    away_rows = xm[pl.ds(pl.multiple_of((1 - core) * hr, hr), hr), :]
    for c in range(0, cols, width):
        s0[:, c:c + width] = jnp.dot(away_rows, w_v[:, c:c + width], preferred_element_type=F32).astype(BF16)
    pair = pltpu.make_async_remote_copy(
        src_ref=s0, dst_ref=t0, send_sem=vsem.at[0], recv_sem=vsem.at[1],
        device_id={"pool": partner_of(0)}, device_id_type=MESH,
    )
    pair.start()
    kept_rows = xm[pl.ds(pl.multiple_of(core * hr, hr), hr), :]
    for c in range(0, cols, width):
        base[:, c:c + width] = jnp.dot(kept_rows, w_v[:, c:c + width], preferred_element_type=F32)

    attend(2, 4)

    each(1, lambda k, to, frm: rank_copy(k, to, frm).wait_recv())
    mine = jnp.sum(rr[...].astype(F32), axis=0).astype(BF16)
    rs[...] = mine
    rv[mt, me // 2] = mine
    for off in range(tensor):
        tt = lax.rem(mt + off, tensor)
        each(1 if off == 0 else 0, lambda k, to, frm: vec_copy(off, k, to, tt, me // 2, mt).start(), half, 2)

    attend(4, 6)

    pair.wait_recv()
    for c in ups:
        c.wait()
    for c in pups:
        c.wait_recv()
    for off in range(tensor):
        tf = lax.rem(mt + tensor - off, tensor)
        each(
            1 if off == 0 else 0,
            lambda k, to, frm: vec_copy(off, k, to, mt, frm // 2, tf).wait_recv(), half, 2,
        )
    pages = pages_ref[...]
    ids_half = ids3[pl.ds(core * half, half)].reshape(hr, LANES)
    vecs = []
    for i, holder in enumerate((me, partner_of(0))):
        adapter = jnp.sum(
            jnp.where(pages == holder, lax.broadcasted_iota(jnp.int32, pages.shape, 1), 0), axis=1, keepdims=True
        )
        for t in range(tensor):
            vec = jnp.where(ids_half == adapter, rv[t].astype(F32).reshape(hr, LANES), 0.0).astype(BF16)
            vecs.append((vec, i, t))

    def hop(g, j):
        sems = ((sx, rx), (sy, ry))[j]
        return pltpu.make_async_remote_copy(
            src_ref=bufs[g][1 + 2 * j], dst_ref=bufs[g][2 + 2 * j],
            send_sem=sems[0].at[g], recv_sem=sems[1].at[g],
            device_id={"pool": partner_of(orders()[g][j])}, device_id_type=MESH,
        )

    zi = me // 8

    def last_copy(g, k):
        to = lax.rem(zi + k, eighth)
        return pltpu.make_async_remote_copy(
            src_ref=bufs[g][5].at[to], dst_ref=bufs[g][6].at[k - 1],
            send_sem=sz.at[g, k], recv_sem=rz.at[g, k],
            device_id={"pool": lax.rem(me, 8) + 8 * to}, device_id_type=MESH,
        )

    offs = []
    for g, (b1, b2) in enumerate(orders()):
        acc, x_out = bufs[g][0], bufs[g][1]
        for c in range(0, gw, width):
            at = slice(g * gw + c, g * gw + c + width)
            part = base[:, at] + t0[:, at].astype(F32)
            for vec, i, t in vecs:
                part = part + ADAPTER_SCALE * jnp.dot(vec, up_v[i, t, :, at], preferred_element_type=F32)
            for n in range(half):
                d = 2 * n
                where = ((d >> b1) & 1) * quarter + ((d >> b2) & 1) * eighth + d // 8
                acc[where, :, c:c + width] = part[n * rd:(n + 1) * rd]
        b = bit_of(me, b1)
        x_out[...] = acc[pl.ds((1 - b) * quarter, quarter)].astype(BF16)
        hop(g, 0).start()
        offs.append(b * quarter)
    attend(6, 7)
    for g, (b1, b2) in enumerate(orders()):
        acc, _, x_in, y_out = bufs[g][:4]
        hop(g, 0).wait_recv()
        b = bit_of(me, b2)
        away, keep = (1 - b) * eighth, b * eighth
        y_out[...] = (acc[pl.ds(offs[g] + away, eighth)] + x_in[pl.ds(away, eighth)].astype(F32)).astype(BF16)
        hop(g, 1).start()
        acc[pl.ds(offs[g] + keep, eighth)] += x_in[pl.ds(keep, eighth)].astype(F32)
        offs[g] = offs[g] + keep
    attend(7, 8)
    for g in range(groups):
        acc, _, _, _, y_in, z_out, _ = bufs[g]
        hop(g, 1).wait_recv()
        full = acc[pl.ds(offs[g], eighth)] + y_in[...].astype(F32)
        acc[pl.ds(offs[g], eighth)] = full
        z_out[...] = full.astype(BF16)
        for k in range(1, eighth):
            last_copy(g, k).start()
    for g in range(groups):
        acc, z_in = bufs[g][0], bufs[g][6]
        for k in range(1, eighth):
            last_copy(g, k).wait_recv()
        done = acc[offs[g] + zi]
        for k in range(1, eighth):
            done = done + z_in[k - 1].astype(F32)
        fresh_ref[:, g * gw:(g + 1) * gw] = done.astype(BF16)

    for h in range(heads):
        new_k = fresh_ref[:, 2 * h * HD:(2 * h + 1) * HD].astype(F32)
        new_v = fresh_ref[:, (2 * h + 1) * HD:(2 * h + 2) * HD].astype(F32)
        for gq in range(GROUP):
            j = h * GROUP + gq
            at = pl.ds(j, rd, stride=nq)
            own = jnp.sum(qs[at, :] * new_k, axis=-1, keepdims=True) * inv_root
            m = m_acc[at, :]
            peak = jnp.maximum(m, own)
            old_w = jnp.exp(m - peak)
            own_w = jnp.exp(own - peak)
            total_w = l_acc[at, :] * old_w + own_w
            mix = o_acc[at, :] * old_w + own_w.astype(BF16).astype(F32) * new_v
            att_ref[:, j * HD:(j + 1) * HD] = (mix / total_w).astype(BF16)

    each(1, lambda k, to, frm: hid_copy(k, to, slot(me)).wait_send())
    for c in pups:
        c.wait_send()
    each(1, lambda k, to, frm: rank_copy(k, to, me).wait_send())
    pair.wait_send()
    for off in range(tensor):
        tt = lax.rem(mt + off, tensor)
        each(1 if off == 0 else 0, lambda k, to, frm: vec_copy(off, k, to, tt, me // 2, mt).wait_send(), half, 2)
    for g in range(groups):
        hop(g, 0).wait_send()
        hop(g, 1).wait_send()
        for k in range(1, eighth):
            last_copy(g, k).wait_send()


def body(pool, tensor, hidden, kv_w, down, up, ids, pages, lens, queries, cache):
    rd, width = hidden.shape
    feats, cols = kv_w.shape
    adapters, rank, _ = down.shape
    lmax = cache.shape[1]
    heads = cols // (2 * HD)
    dma = pltpu.SemaphoreType.DMA
    vm = pltpu.VMEM
    nq = heads * GROUP
    groups = len(orders())
    gw = cols // groups
    half, quarter, eighth = pool // 2, pool // 4, pool // 8
    nup = tensor * (LANES // rank)
    scratch = [
        vm((pool, rd, feats), BF16),
        vm((pool * rd, feats), BF16),
        vm((feats, cols), BF16),
        vm((adapters * rank, feats), BF16),
        vm((2, tensor, LANES, cols), BF16),
        vm((rd, lmax, cols), BF16),
        vm((rd, queries.shape[1]), BF16),
        vm((1, pool * rd), jnp.int32),
        vm((1, adapters), jnp.int32),
        pltpu.SMEM((rd,), jnp.int32),
        vm((pool, rd, LANES), jnp.int32),
        vm((rd * nq, HD), F32),
        vm((rd * nq, HD), F32),
        vm((rd * nq, LANES), F32),
        vm((rd * nq, LANES), F32),
        vm((pool, rd, LANES), BF16),
        vm((pool, rd, LANES), BF16),
        vm((rd, LANES), BF16),
        vm((tensor, half, rd, LANES), BF16),
        vm((half * rd, cols), F32),
        vm((half * rd, cols), BF16),
        vm((half * rd, cols), BF16),
    ]
    for _ in range(groups):
        scratch += [vm((half, rd, gw), F32)]
        scratch += [vm((quarter, rd, gw), BF16)] * 2
        scratch += [vm((eighth, rd, gw), BF16)] * 2
        scratch += [vm((eighth, rd, gw), BF16), vm((eighth - 1, rd, gw), BF16)]
    scratch += [
        dma((7,)), dma((rd,)), dma((nup,)), dma((2,)),
        dma((pool,)), dma((pool,)),
        dma((pool,)), dma((pool,)),
        dma((tensor, half)), dma((tensor, half)),
        dma((nup,)), dma((nup,)),
        dma((groups,)), dma((groups,)),
        dma((groups,)), dma((groups,)),
        dma((groups, eighth)), dma((groups, eighth)),
    ]
    vspec = pl.BlockSpec(memory_space=pltpu.VMEM)
    hbm = pl.BlockSpec(memory_space=pl.ANY)
    return pl.pallas_call(
        functools.partial(kernel, pool, tensor, rd, feats, cols, rank, lmax, heads),
        out_shape=(
            jax.ShapeDtypeStruct((rd, cols), BF16),
            jax.ShapeDtypeStruct((rd, queries.shape[1]), BF16),
        ),
        in_specs=[hbm] * 9,
        out_specs=(vspec, vspec),
        scratch_shapes=scratch,
        compiler_params=pltpu.CompilerParams(
            collective_id=0, has_side_effects=True, vmem_limit_bytes=60 * 1024 * 1024
        ),
    )(
        hidden, ids.reshape(1, -1), pages.reshape(1, -1), lens, queries,
        kv_w, down.reshape(adapters * rank, feats), up.reshape(up.shape[1], cols), cache,
    )


def solution(mesh):
    in_specs = (
        P(("groups", "pool"), None),
        P("pool", "tensor"),
        P("groups", "tensor", "pool"),
        P(("groups", "pool"), None, "tensor"),
        P("groups", None),
        P("groups"),
        P(("groups", "pool")),
        P(("groups", "pool"), "tensor"),
        P(("groups", "pool"), None, "tensor"),
    )
    out_specs = (P(("groups", "pool"), "tensor"), P(("groups", "pool"), "tensor"))
    fn = functools.partial(body, mesh.shape["pool"], mesh.shape["tensor"])
    return jax.shard_map(fn, mesh=mesh, in_specs=in_specs, out_specs=out_specs, check_vma=False)
```

```python
import functools
import math

import jax
import jax.numpy as jnp
from jax import lax
from jax.experimental import pallas as pl
from jax.experimental.pallas import tpu as pltpu
from jax.sharding import PartitionSpec as P

QH = 64
KVH = 8
HD = 128
GROUP = QH // KVH
LANES = 128
ADAPTER_SCALE = 0.5
MESH = pl.DeviceIdType.MESH
BF16 = jnp.bfloat16
F32 = jnp.float32


def orders():
    return ((1, 2), (2, 1), (1, 2), (2, 1))


def kernel(pool, tensor, rd, feats, cols, rank, lmax, heads, *refs):
    hidden, ids_hbm, pages_hbm, lens_hbm, q_hbm, w_hbm, down_hbm, up_hbm, cache_hbm = refs[:9]
    fresh_ref, att_ref = refs[9:11]
    (xg, xm, w_v, down_v, up_v, kv, q_ref, ids_raw, pages_ref, lens_ref, ids3, qs, o_acc, m_acc, l_acc,
     rk, rr, rs, rv, base, s0, t0) = refs[11:33]
    groups = len(orders())
    gw = cols // groups
    per = 7
    bufs = [refs[33 + g * per:33 + (g + 1) * per] for g in range(groups)]
    (lsem, kvsem, usem, vsem, s1, r1, s2, r2, s3, r3, sp, rp, sx, rx, sy, ry, sz, rz) = refs[33 + groups * per:]

    me = lax.axis_index("pool")
    mt = lax.axis_index("tensor")
    rows = pool * rd
    half, quarter, eighth = pool // 2, pool // 4, pool // 8
    copies_up = LANES // rank
    hr = half * rd

    def bit_of(d, b):
        return lax.rem(d // (1 << b), 2)

    def partner_of(b):
        return me + (1 - 2 * bit_of(me, b)) * (1 << b)

    core = bit_of(me, 0)

    def slot(d):
        return lax.rem(d, 2) * half + d // 2

    barrier = pltpu.get_barrier_semaphore()
    for to in range(tensor):
        tt = lax.rem(mt + to, tensor)

        def greet(k, carry, tt=tt):
            pl.semaphore_signal(
                barrier, inc=1, device_id={"pool": lax.rem(me + k, pool), "tensor": tt}, device_id_type=MESH
            )
            return carry

        lax.fori_loop(1 if to == 0 else 0, pool, greet, 0)

    def hidden_cols(d):
        return hidden.at[:, pl.ds(pl.multiple_of(d * feats, feats), feats)]

    own_x = pltpu.make_async_copy(hidden_cols(me), xg.at[slot(me)], lsem.at[0])
    c_q = pltpu.make_async_copy(q_hbm, q_ref, lsem.at[1])
    c_ids = pltpu.make_async_copy(ids_hbm, ids_raw, lsem.at[2])
    c_pages = pltpu.make_async_copy(pages_hbm, pages_ref, lsem.at[3])
    c_lens = pltpu.make_async_copy(lens_hbm, lens_ref, lsem.at[4])
    c_down = pltpu.make_async_copy(down_hbm, down_v, lsem.at[5])
    c_w = pltpu.make_async_copy(w_hbm, w_v, lsem.at[6])
    ups = []
    pups = []
    for t in range(tensor):
        for i in range(copies_up):
            src = up_hbm.at[pl.ds(t * rank, rank)]
            n = t * copies_up + i
            ups.append(pltpu.make_async_copy(src, up_v.at[0, t, pl.ds(i * rank, rank)], usem.at[n]))
            pups.append(
                pltpu.make_async_remote_copy(
                    src_ref=src, dst_ref=up_v.at[1, t, pl.ds(i * rank, rank)],
                    send_sem=sp.at[n], recv_sem=rp.at[n],
                    device_id={"pool": partner_of(0)}, device_id_type=MESH,
                )
            )
    kvs = [pltpu.make_async_copy(cache_hbm.at[r], kv.at[r], kvsem.at[r]) for r in range(rd)]
    for c in [own_x, c_q, c_ids, c_pages, c_lens, c_down, c_w] + kvs[:2]:
        c.start()

    pl.semaphore_wait(barrier, pool * tensor - 1)

    def hid_copy(k, to, at):
        return pltpu.make_async_remote_copy(
            src_ref=hidden_cols(to), dst_ref=xg.at[at], send_sem=s1.at[k], recv_sem=r1.at[k],
            device_id={"pool": to}, device_id_type=MESH,
        )

    def rank_copy(k, to, at):
        return pltpu.make_async_remote_copy(
            src_ref=rk.at[slot(to)], dst_ref=rr.at[at], send_sem=s2.at[k], recv_sem=r2.at[k],
            device_id={"pool": to}, device_id_type=MESH,
        )

    def vec_copy(off, k, to, tt, at, ts):
        return pltpu.make_async_remote_copy(
            src_ref=rs, dst_ref=rv.at[ts, at], send_sem=s3.at[off, k], recv_sem=r3.at[off, k],
            device_id={"pool": to, "tensor": tt}, device_id_type=MESH,
        )

    def each(first, fn, count=pool, stride=1):
        def step(k, carry):
            fn(k, lax.rem(me + k * stride, pool), lax.rem(me + pool - k * stride, pool))
            return carry

        lax.fori_loop(first, count, step, 0)

    each(1, lambda k, to, frm: hid_copy(k, to, slot(me)).start())
    for c in pups + ups + kvs[2:]:
        c.start()

    nq = heads * GROUP
    c_q.wait()
    for j in range(nq):
        qs[pl.ds(j, rd, stride=nq), :] = q_ref[:, j * HD:(j + 1) * HD].astype(F32)
    inv_root = 1.0 / math.sqrt(HD)
    c_ids.wait()
    ids_t = jnp.broadcast_to(ids_raw[...], (LANES, rows)).T
    for d in range(pool):
        ids3[(d % 2) * half + d // 2] = ids_t[d * rd:(d + 1) * rd]
    c_pages.wait()
    c_lens.wait()

    def attend(r0, r1_):
        for r in range(r0, r1_):
            kvs[r].wait()

        def row(r, carry):
            live = lax.broadcasted_iota(jnp.int32, (nq, lmax), 1) < lens_ref[r]
            q_row = qs[pl.ds(pl.multiple_of(r * nq, nq), nq), :].astype(BF16)
            parts = []
            for h in range(heads):
                k_h = kv[r, :, 2 * h * HD:(2 * h + 1) * HD]
                parts.append(
                    lax.dot_general(
                        q_row[h * GROUP:(h + 1) * GROUP], k_h, (((1,), (1,)), ((), ())),
                        preferred_element_type=F32,
                    )
                )
            s = jnp.concatenate(parts, axis=0) * inv_root
            s = jnp.where(live, s, -jnp.inf)
            m = jnp.max(s, axis=-1, keepdims=True)
            p = jnp.exp(s - m)
            l = jnp.sum(p, axis=-1, keepdims=True)
            pb = p.astype(BF16)
            outs = []
            for h in range(heads):
                v_h = kv[r, :, (2 * h + 1) * HD:(2 * h + 2) * HD]
                outs.append(
                    jnp.dot(pb[h * GROUP:(h + 1) * GROUP], v_h, preferred_element_type=F32)
                )
            at = pl.ds(pl.multiple_of(r * nq, nq), nq)
            o_acc[at, :] = jnp.concatenate(outs, axis=0)
            m_acc[at, :] = jnp.broadcast_to(m, (nq, LANES))
            l_acc[at, :] = jnp.broadcast_to(l, (nq, LANES))
            return carry

        lax.fori_loop(r0, r1_, row, 0)

    c_down.wait()
    c_w.wait()
    attend(0, 2)

    own_x.wait()
    each(1, lambda k, to, frm: hid_copy(k, to, slot(frm)).wait_recv())
    xm[...] = xg[...].astype(F32).reshape(rows, feats).astype(BF16)
    ids = ids3[...].reshape(rows, LANES)
    total = jnp.zeros((rows, LANES), F32)
    lane_sub = lax.broadcasted_iota(jnp.int32, (rows, LANES), 1) // rank
    for c in range(down_v.shape[0] // LANES):
        y = lax.dot_general(
            xm[...], down_v[c * LANES:(c + 1) * LANES, :], (((1,), (1,)), ((), ())),
            preferred_element_type=F32,
        )
        total = total + jnp.where(lane_sub + c * copies_up == ids, y, 0.0)
    rk[...] = total.reshape(pool, rd, LANES).astype(BF16)
    rr[me] = rk[slot(me)]
    each(1, lambda k, to, frm: rank_copy(k, to, me).start())

    width = 256
    away_rows = xm[pl.ds(pl.multiple_of((1 - core) * hr, hr), hr), :]
    for c in range(0, cols, width):
        s0[:, c:c + width] = jnp.dot(away_rows, w_v[:, c:c + width], preferred_element_type=F32).astype(BF16)
    pair = pltpu.make_async_remote_copy(
        src_ref=s0, dst_ref=t0, send_sem=vsem.at[0], recv_sem=vsem.at[1],
        device_id={"pool": partner_of(0)}, device_id_type=MESH,
    )
    pair.start()
    kept_rows = xm[pl.ds(pl.multiple_of(core * hr, hr), hr), :]
    for c in range(0, cols, width):
        base[:, c:c + width] = jnp.dot(kept_rows, w_v[:, c:c + width], preferred_element_type=F32)

    attend(2, 5)

    each(1, lambda k, to, frm: rank_copy(k, to, frm).wait_recv())
    mine = jnp.sum(rr[...].astype(F32), axis=0).astype(BF16)
    rs[...] = mine
    rv[mt, me // 2] = mine
    for off in range(tensor):
        tt = lax.rem(mt + off, tensor)
        each(1 if off == 0 else 0, lambda k, to, frm: vec_copy(off, k, to, tt, me // 2, mt).start(), half, 2)

    attend(5, 7)

    pair.wait_recv()
    for c in ups:
        c.wait()
    for c in pups:
        c.wait_recv()
    for off in range(tensor):
        tf = lax.rem(mt + tensor - off, tensor)
        each(
            1 if off == 0 else 0,
            lambda k, to, frm: vec_copy(off, k, to, mt, frm // 2, tf).wait_recv(), half, 2,
        )
    pages = pages_ref[...]
    ids_half = ids3[pl.ds(core * half, half)].reshape(hr, LANES)
    vecs = []
    for i, holder in enumerate((me, partner_of(0))):
        adapter = jnp.sum(
            jnp.where(pages == holder, lax.broadcasted_iota(jnp.int32, pages.shape, 1), 0), axis=1, keepdims=True
        )
        for t in range(tensor):
            vec = jnp.where(ids_half == adapter, rv[t].astype(F32).reshape(hr, LANES), 0.0).astype(BF16)
            vecs.append((vec, i, t))

    def hop(g, j):
        sems = ((sx, rx), (sy, ry))[j]
        return pltpu.make_async_remote_copy(
            src_ref=bufs[g][1 + 2 * j], dst_ref=bufs[g][2 + 2 * j],
            send_sem=sems[0].at[g], recv_sem=sems[1].at[g],
            device_id={"pool": partner_of(orders()[g][j])}, device_id_type=MESH,
        )

    zi = me // 8

    def last_copy(g, k):
        to = lax.rem(zi + k, eighth)
        return pltpu.make_async_remote_copy(
            src_ref=bufs[g][5].at[to], dst_ref=bufs[g][6].at[k - 1],
            send_sem=sz.at[g, k], recv_sem=rz.at[g, k],
            device_id={"pool": lax.rem(me, 8) + 8 * to}, device_id_type=MESH,
        )

    def join(h0, h1):
        for h in range(h0, h1):
            new_k = fresh_ref[:, 2 * h * HD:(2 * h + 1) * HD].astype(F32)
            new_v = fresh_ref[:, (2 * h + 1) * HD:(2 * h + 2) * HD].astype(F32)
            for gq in range(GROUP):
                j = h * GROUP + gq
                at = pl.ds(j, rd, stride=nq)
                own = jnp.sum(qs[at, :] * new_k, axis=-1, keepdims=True) * inv_root
                m = m_acc[at, :]
                peak = jnp.maximum(m, own)
                old_w = jnp.exp(m - peak)
                own_w = jnp.exp(own - peak)
                total_w = l_acc[at, :] * old_w + own_w
                mix = o_acc[at, :] * old_w + own_w.astype(BF16).astype(F32) * new_v
                att_ref[:, j * HD:(j + 1) * HD] = (mix / total_w).astype(BF16)

    offs = []
    for g, (b1, b2) in enumerate(orders()):
        acc, x_out = bufs[g][0], bufs[g][1]
        for c in range(0, gw, width):
            at = slice(g * gw + c, g * gw + c + width)
            part = base[:, at] + t0[:, at].astype(F32)
            for vec, i, t in vecs:
                part = part + ADAPTER_SCALE * jnp.dot(vec, up_v[i, t, :, at], preferred_element_type=F32)
            for n in range(half):
                d = 2 * n
                where = ((d >> b1) & 1) * quarter + ((d >> b2) & 1) * eighth + d // 8
                acc[where, :, c:c + width] = part[n * rd:(n + 1) * rd]
        b = bit_of(me, b1)
        x_out[...] = acc[pl.ds((1 - b) * quarter, quarter)].astype(BF16)
        hop(g, 0).start()
        offs.append(b * quarter)
    attend(7, 8)
    each(1, lambda k, to, frm: hid_copy(k, to, slot(me)).wait_send())
    for c in pups:
        c.wait_send()
    each(1, lambda k, to, frm: rank_copy(k, to, me).wait_send())
    pair.wait_send()
    for off in range(tensor):
        tt = lax.rem(mt + off, tensor)
        each(1 if off == 0 else 0, lambda k, to, frm: vec_copy(off, k, to, tt, me // 2, mt).wait_send(), half, 2)
    for g, (b1, b2) in enumerate(orders()):
        acc, _, x_in, y_out = bufs[g][:4]
        hop(g, 0).wait_recv()
        b = bit_of(me, b2)
        away, keep = (1 - b) * eighth, b * eighth
        y_out[...] = (acc[pl.ds(offs[g] + away, eighth)] + x_in[pl.ds(away, eighth)].astype(F32)).astype(BF16)
        hop(g, 1).start()
        acc[pl.ds(offs[g] + keep, eighth)] += x_in[pl.ds(keep, eighth)].astype(F32)
        offs[g] = offs[g] + keep
    for g in range(groups):
        acc, _, _, _, y_in, z_out, _ = bufs[g]
        hop(g, 1).wait_recv()
        full = acc[pl.ds(offs[g], eighth)] + y_in[...].astype(F32)
        acc[pl.ds(offs[g], eighth)] = full
        z_out[...] = full.astype(BF16)
        for k in range(1, eighth):
            last_copy(g, k).start()
    for g in range(groups):
        acc, z_in = bufs[g][0], bufs[g][6]
        for k in range(1, eighth):
            last_copy(g, k).wait_recv()
        done = acc[offs[g] + zi]
        for k in range(1, eighth):
            done = done + z_in[k - 1].astype(F32)
        fresh_ref[:, g * gw:(g + 1) * gw] = done.astype(BF16)
        join(g * heads // groups, (g + 1) * heads // groups)

    for g in range(groups):
        hop(g, 0).wait_send()
        hop(g, 1).wait_send()
        for k in range(1, eighth):
            last_copy(g, k).wait_send()


def body(pool, tensor, hidden, kv_w, down, up, ids, pages, lens, queries, cache):
    rd, width = hidden.shape
    feats, cols = kv_w.shape
    adapters, rank, _ = down.shape
    lmax = cache.shape[1]
    heads = cols // (2 * HD)
    dma = pltpu.SemaphoreType.DMA
    vm = pltpu.VMEM
    nq = heads * GROUP
    groups = len(orders())
    gw = cols // groups
    half, quarter, eighth = pool // 2, pool // 4, pool // 8
    nup = tensor * (LANES // rank)
    scratch = [
        vm((pool, rd, feats), BF16),
        vm((pool * rd, feats), BF16),
        vm((feats, cols), BF16),
        vm((adapters * rank, feats), BF16),
        vm((2, tensor, LANES, cols), BF16),
        vm((rd, lmax, cols), BF16),
        vm((rd, queries.shape[1]), BF16),
        vm((1, pool * rd), jnp.int32),
        vm((1, adapters), jnp.int32),
        pltpu.SMEM((rd,), jnp.int32),
        vm((pool, rd, LANES), jnp.int32),
        vm((rd * nq, HD), F32),
        vm((rd * nq, HD), F32),
        vm((rd * nq, LANES), F32),
        vm((rd * nq, LANES), F32),
        vm((pool, rd, LANES), BF16),
        vm((pool, rd, LANES), BF16),
        vm((rd, LANES), BF16),
        vm((tensor, half, rd, LANES), BF16),
        vm((half * rd, cols), F32),
        vm((half * rd, cols), BF16),
        vm((half * rd, cols), BF16),
    ]
    for _ in range(groups):
        scratch += [vm((half, rd, gw), F32)]
        scratch += [vm((quarter, rd, gw), BF16)] * 2
        scratch += [vm((eighth, rd, gw), BF16)] * 2
        scratch += [vm((eighth, rd, gw), BF16), vm((eighth - 1, rd, gw), BF16)]
    scratch += [
        dma((7,)), dma((rd,)), dma((nup,)), dma((2,)),
        dma((pool,)), dma((pool,)),
        dma((pool,)), dma((pool,)),
        dma((tensor, half)), dma((tensor, half)),
        dma((nup,)), dma((nup,)),
        dma((groups,)), dma((groups,)),
        dma((groups,)), dma((groups,)),
        dma((groups, eighth)), dma((groups, eighth)),
    ]
    vspec = pl.BlockSpec(memory_space=pltpu.VMEM)
    hbm = pl.BlockSpec(memory_space=pl.ANY)
    return pl.pallas_call(
        functools.partial(kernel, pool, tensor, rd, feats, cols, rank, lmax, heads),
        out_shape=(
            jax.ShapeDtypeStruct((rd, cols), BF16),
            jax.ShapeDtypeStruct((rd, queries.shape[1]), BF16),
        ),
        in_specs=[hbm] * 9,
        out_specs=(vspec, vspec),
        scratch_shapes=scratch,
        compiler_params=pltpu.CompilerParams(
            collective_id=0, has_side_effects=True, vmem_limit_bytes=60 * 1024 * 1024
        ),
    )(
        hidden, ids.reshape(1, -1), pages.reshape(1, -1), lens, queries,
        kv_w, down.reshape(adapters * rank, feats), up.reshape(up.shape[1], cols), cache,
    )


def solution(mesh):
    in_specs = (
        P(("groups", "pool"), None),
        P("pool", "tensor"),
        P("groups", "tensor", "pool"),
        P(("groups", "pool"), None, "tensor"),
        P("groups", None),
        P("groups"),
        P(("groups", "pool")),
        P(("groups", "pool"), "tensor"),
        P(("groups", "pool"), None, "tensor"),
    )
    out_specs = (P(("groups", "pool"), "tensor"), P(("groups", "pool"), "tensor"))
    fn = functools.partial(body, mesh.shape["pool"], mesh.shape["tensor"])
    return jax.shard_map(fn, mesh=mesh, in_specs=in_specs, out_specs=out_specs, check_vma=False)
```
